1024 devices in a mesh: fsdp: 128 (over z_lo, x, core), parity: 8 (over y, z_hi).
Axes of the slice: x: 4, y: 4, z: 32 (z_hi: 2, z_lo: 16; z = z_hi * 16 + z_lo), core: 2. Of those that a mesh axis runs over, the one named last changes fastest.
Arguments:
- param: float32 [8, 8388608], P('parity', 'fsdp'), may hold values from -0.3 to 0.3
- first_moment: float32 [8, 8388608], P('parity', 'fsdp'), may hold values from -0.0006 to 0.0006
- second_moment: float32 [8, 8388608], P('parity', 'fsdp'), may hold values from 1e-09 to 1e-07
- grad: bfloat16 [8, 8388608], P('parity', 'fsdp')
- saved_param: float32 [8, 8388608], P('parity', 'fsdp'), may hold values from -0.3 to 0.3
- owner: int32 [8], replicated, may hold values from 0 to 7, each once
- generator: float32 [8, 8], replicated, may hold values from -1 to 1, as said below
Outputs:
- new_param: float32 [8, 8388608], P('parity', 'fsdp')
- new_first: float32 [8, 8388608], P('parity', 'fsdp')
- new_second: float32 [8, 8388608], P('parity', 'fsdp')
- parity_rows: float32 [8, 8388608], P('parity', 'fsdp')
The draws below stay inside these ranges and needn't reach their ends.
Inputs may be any that keep to these rules, and one draw needn't show every extreme that they name: owner is a permutation of the 8 code rows. generator[k, j] is the k-th power of a node of member j; the nodes are distinct.
All inputs are finite; a program needn't handle non-finite values.
Results may differ from the reference program's by a relative error of at most 0.0065.
Values may be sent and summed in bfloat16 or wider, within the bound.
A program may use at most 32 MiB of HBM per device.

```python
import math
import jax
import jax.numpy as jnp

SHARD = 65536
COLS = 8388608
N_PARITY = 8


def draw_grad(key, part):
    key = jax.random.fold_in(key, 11)
    key_base, key_row, key_block, key_cell = jax.random.split(key, 4)
    blocks = COLS // SHARD
    rise_block = 3.0 ** (jnp.arange(blocks, dtype=jnp.float32) / max(blocks - 1, 1))
    rise_row = 1.0 + 2.0 * jnp.arange(N_PARITY, dtype=jnp.float32) / max(N_PARITY - 1, 1)
    top = 10.0
    scale = 0.01
    base = jnp.clip(jax.random.normal(key_base, (N_PARITY, blocks, SHARD), jnp.float32), -6.0, 6.0)
    row_loud = jnp.exp(jax.random.uniform(key_row, (N_PARITY, 1, 1), jnp.float32) * jnp.log(top))
    block_loud = jnp.exp(jax.random.uniform(key_block, (1, blocks, 1), jnp.float32) * jnp.log(top))
    cell_loud = jnp.exp(jax.random.uniform(key_cell, (N_PARITY, blocks, 1), jnp.float32) * jnp.log(2.0))
    rises = rise_row[:, None, None] * rise_block[None, :, None]
    values = scale * base * row_loud * block_loud * cell_loud * rises
    return values.reshape(N_PARITY, COLS).astype(jnp.bfloat16)


def draw_generator(key, part):
    key = jax.random.fold_in(key, 23)
    jitter = jax.random.uniform(key, (N_PARITY,), jnp.float32, 0.2, 0.8)
    nodes = (jnp.arange(N_PARITY, dtype=jnp.float32) + jitter) / N_PARITY * 2.0 - 1.0
    powers = jnp.arange(N_PARITY, dtype=jnp.float32)[:, None]
    return jnp.power(nodes[None, :], powers)


def steps_of(own_key, extent, cuts, low, largest):
    factor_of, own = 1.0, jax.random.fold_in(own_key, 6)
    for axis_at, blocks in cuts:
        steps = jnp.exp(jax.random.uniform(jax.random.fold_in(own, axis_at), (blocks,), jnp.float32, low / len(cuts), largest / len(cuts)))
        factor_of = factor_of * jnp.repeat(steps, extent[axis_at] // blocks).reshape([-1 if axis == axis_at else 1 for axis in range(len(extent))])
    return factor_of


def gaussian(key, extent, width, bound, cuts=(), kind=jnp.bfloat16):
    array = jax.random.normal(key, extent, jnp.float32) * width
    if len(cuts) > 0:
        array = steps_of(key, extent, cuts, -0.22, 0.18) * array
    return jnp.clip(array, min=-bound, max=bound).astype(kind)


def setup_inputs(seed: int = 0) -> dict:
    arg_keys = jax.random.split(jax.random.key(seed), 8)
    return {
        "param": gaussian(arg_keys[0], (N_PARITY, COLS), 0.05, 0.3, ((0, 8), (1, 128)), jnp.float32),
        "first_moment": gaussian(arg_keys[1], (N_PARITY, COLS), 0.0001, 0.0006, ((0, 8), (1, 128)), jnp.float32),
        "second_moment": jnp.clip(jnp.exp(math.log(1.0000000116860974e-07) - 4.6051702 * jax.random.uniform(arg_keys[2], (N_PARITY, COLS), jnp.float32) ** steps_of(arg_keys[2], (N_PARITY, COLS), ((0, 8), (1, 128)), -0.2, 0.2)), 9.999999717180685e-10, 1.0000000116860974e-07),
        "grad": draw_grad(jax.random.fold_in(arg_keys[7], 71), 0),
        "saved_param": gaussian(arg_keys[4], (N_PARITY, COLS), 0.05, 0.3, ((0, 8), (1, 128)), jnp.float32),
        "owner": jax.random.permutation(arg_keys[5], N_PARITY).astype(jnp.int32),
        "generator": draw_generator(jax.random.fold_in(arg_keys[7], 71), 0),
    }


def reference(param, first_moment, second_moment, grad, saved_param, owner, generator):
    grad_f = grad.astype(jnp.float32)
    norm = jnp.sqrt(jnp.sum(grad_f * grad_f))
    factor = jnp.minimum(1.0, 1.0 / (norm + 1e-06))
    clipped = grad_f * factor
    new_first = 0.9 * first_moment + 0.1 * clipped
    new_second = 0.95 * second_moment + 0.05 * clipped * clipped
    update = new_first / (1.0 - 0.9 ** 10) / (jnp.sqrt(new_second / (1.0 - 0.95 ** 10)) + 1e-08) + 0.1 * param
    new_param = param - 0.05 * update
    delta = (new_param - saved_param).astype(jnp.bfloat16).astype(jnp.float32)
    rows_gen = generator[owner]
    parity_rows = jnp.dot(rows_gen, delta, precision=jax.lax.Precision.HIGHEST)
    return (new_param, new_first, new_second, parity_rows)
```

```python
import functools

import jax
import jax.numpy as jnp
from jax import lax
from jax.experimental import pallas as pl
from jax.experimental.pallas import tpu as pltpu
from jax.sharding import PartitionSpec as P

MESH = pl.DeviceIdType.MESH
NX, NY, NZ, NC = 4, 4, 32, 2
HALF = NZ // 2
REACH = NZ // 4
LANES = 128


def position():
    f = lax.axis_index("fsdp")
    p = lax.axis_index("parity")
    x = lax.rem(lax.div(f, NC), NX)
    z = lax.rem(p, 2) * HALF + lax.div(f, NX * NC)
    return x, lax.div(p, 2), z, lax.rem(f, NC)


def device(x, y, z, c):
    return ((lax.rem(z, HALF) * NX + x) * NC + c, y * 2 + lax.div(z, HALF))


def kernel(
    param, first, second, grad, saved, owner, gen,
    out_param, out_first, out_second, out_rows,
    g_v, p_v, m_v, v_v, s_v, np_v, nm_v, nv_v, rows_v, deltas,
    plane_buf, near_buf, far_buf,
    in_sem, out_sem, norm_send, norm_recv,
    z_send, z_recv, y_send, y_recv,
    *, chunks,
):
    x, y, z, c = position()
    me = lax.axis_index("parity")
    other = y * 2 + lax.rem(lax.axis_index("parity") + 1, 2)
    rows = p_v.shape[0]
    step = rows // chunks

    loads = [
        pltpu.make_async_copy(src, dst, in_sem.at[i])
        for i, (src, dst) in enumerate(
            ((grad, g_v), (param, p_v), (first, m_v), (second, v_v), (saved, s_v))
        )
    ]
    for load in loads:
        load.start()

    def along_z(k):
        return device(x, y, lax.rem(z + k + NZ, NZ), c)

    in_plane = NX * NY * NC
    mine = (x * NY + y) * NC + c

    def plane_device(j):
        return device(lax.div(j, NY * NC), lax.rem(lax.div(j, NC), NY), z, lax.rem(j, NC))

    barrier = pltpu.get_barrier_semaphore()

    def hail_z(i, _):
        for k in (REACH - i, i - REACH):
            pl.semaphore_signal(barrier, inc=1, device_id=along_z(k), device_id_type=MESH)
        return 0

    lax.fori_loop(0, REACH, hail_z, 0)

    def hail_plane(i, _):
        pl.semaphore_signal(
            barrier, inc=1, device_id=plane_device(lax.rem(mine + i + 1, in_plane)), device_id_type=MESH
        )
        return 0

    lax.fori_loop(0, in_plane - 1, hail_plane, 0)

    loads[0].wait()
    g = g_v[...].astype(jnp.float32)
    squares = jnp.sum(g * g, axis=0, keepdims=True)
    plane_buf[mine] = squares
    pl.semaphore_wait(barrier, 2 * REACH + in_plane - 1)

    def send_plane(i, _):
        pltpu.make_async_remote_copy(
            src_ref=plane_buf.at[mine], dst_ref=plane_buf.at[mine],
            send_sem=norm_send.at[0], recv_sem=norm_recv.at[0],
            device_id=plane_device(lax.rem(mine + i + 1, in_plane)), device_id_type=MESH,
        ).start()
        return 0

    def await_bytes(ref, sem):
        pltpu.make_async_copy(ref, ref, sem).wait()

    lax.fori_loop(0, in_plane - 1, send_plane, 0, unroll=True)
    await_bytes(plane_buf.at[pl.ds(0, in_plane - 1)], norm_recv.at[0])
    plane = jnp.sum(plane_buf[...], axis=0)

    near_buf[REACH - 1] = plane
    for k in (REACH, *(s * d for d in range(REACH - 1, 0, -1) for s in (1, -1))):
        pltpu.make_async_remote_copy(
            src_ref=near_buf.at[REACH - 1], dst_ref=near_buf.at[REACH - 1 + k],
            send_sem=norm_send.at[1], recv_sem=norm_recv.at[1],
            device_id=along_z(-k), device_id_type=MESH,
        ).start()
    await_bytes(near_buf.at[pl.ds(0, 2 * REACH - 1)], norm_recv.at[1])
    above = jnp.sum(near_buf[REACH - 1 :], axis=0)
    below = jnp.sum(near_buf[:REACH], axis=0)
    around = jnp.sum(near_buf[: 2 * REACH - 1], axis=0)
    far_buf[0] = above
    far_buf[1] = below
    for i, k in ((0, -REACH), (1, REACH)):
        pltpu.make_async_remote_copy(
            src_ref=far_buf.at[i], dst_ref=far_buf.at[2 + i],
            send_sem=norm_send.at[2], recv_sem=norm_recv.at[2],
            device_id=along_z(k), device_id_type=MESH,
        ).start()
    for load in loads[1:]:
        load.wait()
    await_bytes(far_buf.at[pl.ds(0, 2)], norm_recv.at[2])
    total = jnp.sum(around + far_buf[2] + far_buf[3], axis=1, keepdims=True)
    norm = jnp.sqrt(total)
    factor = jnp.minimum(1.0, 1.0 / (norm + 1e-6))

    scale_first = 1.0 / (1.0 - 0.9**10)
    scale_second = 1.0 / (1.0 - 0.95**10)

    def y_copy(hop, d, k, slot):
        part = deltas.at[slot, pl.ds(k * step, step)]
        return pltpu.make_async_remote_copy(
            src_ref=part, dst_ref=part,
            send_sem=y_send.at[hop, d - 1, k], recv_sem=y_recv.at[hop, d - 1, k],
            device_id=device(x, lax.rem(y + d, NY), z, c), device_id_type=MESH,
        )

    z_copies, y_copies = [], []
    for k in range(chunks):
        part = pl.ds(k * step, step)
        p = p_v[part]
        clipped = g_v[part].astype(jnp.float32) * factor
        new_first = 0.9 * m_v[part] + 0.1 * clipped
        new_second = 0.95 * v_v[part] + 0.05 * clipped * clipped
        update = new_first * scale_first / (jnp.sqrt(new_second * scale_second) + 1e-8) + 0.1 * p
        new_param = p - 0.05 * update
        np_v[part] = new_param
        nm_v[part] = new_first
        nv_v[part] = new_second
        deltas[me, part] = (new_param - s_v[part]).astype(jnp.bfloat16)
        own = deltas.at[me, part]
        z_copy = pltpu.make_async_remote_copy(
            src_ref=own, dst_ref=own, send_sem=z_send.at[k], recv_sem=z_recv.at[k],
            device_id=along_z(HALF), device_id_type=MESH,
        )
        z_copy.start()
        z_copies.append(z_copy)
    for k in range(chunks):
        for d in (2, 1, 3):
            copy = y_copy(0, d, k, me)
            copy.start()
            y_copies.append(copy)
    stores = [
        pltpu.make_async_copy(src, dst, out_sem.at[i])
        for i, (src, dst) in enumerate(
            ((np_v, out_param), (nm_v, out_first), (nv_v, out_second), (rows_v, out_rows))
        )
    ]
    for store in stores[:3]:
        store.start()

    row = owner[me]
    coefs = [gen[row, j] for j in range(2 * NY)]
    for copy in y_copies:
        copy.wait_recv()
    for k in range(chunks):
        z_copies[k].wait_recv()
        for d in (2, 1, 3):
            copy = y_copy(1, d, k, other)
            copy.start()
            y_copies.append(copy)
    for k in range(chunks):
        part = pl.ds(k * step, step)
        for d in range(3):
            y_copies[3 * chunks + 3 * k + d].wait_recv()
        acc = coefs[0] * deltas[0, part].astype(jnp.float32)
        for j in range(1, 2 * NY):
            acc += coefs[j] * deltas[j, part].astype(jnp.float32)
        rows_v[part] = acc
    stores[3].start()
    await_bytes(plane_buf.at[pl.ds(0, in_plane - 1)], norm_send.at[0])
    await_bytes(near_buf.at[pl.ds(0, 2 * REACH - 1)], norm_send.at[1])
    await_bytes(far_buf.at[pl.ds(0, 2)], norm_send.at[2])
    for copy in z_copies + y_copies:
        copy.wait_send()
    for store in stores:
        store.wait()


def shards(param, first_moment, second_moment, grad, saved_param, owner, generator):
    chunks = 4
    shape = param.shape
    rows = shape[1] // LANES
    tall = lambda a: a.reshape(rows, LANES)
    f32 = jax.ShapeDtypeStruct((rows, LANES), jnp.float32)
    big = pltpu.VMEM((rows, LANES), jnp.float32)
    dma = pltpu.SemaphoreType.DMA
    anywhere = pl.BlockSpec(memory_space=pl.ANY)
    smem = pl.BlockSpec(memory_space=pltpu.SMEM)
    outs = pl.pallas_call(
        functools.partial(kernel, chunks=chunks),
        out_shape=[f32] * 4,
        in_specs=[anywhere] * 5 + [smem] * 2,
        out_specs=[anywhere] * 4,
        scratch_shapes=[
            pltpu.VMEM((rows, LANES), grad.dtype), big, big, big, big, big, big, big, big,
            pltpu.VMEM((2 * NY, rows, LANES), jnp.bfloat16),
            pltpu.VMEM((NX * NY * NC, 1, LANES), jnp.float32),
            pltpu.VMEM((2 * REACH, 1, LANES), jnp.float32),
            pltpu.VMEM((4, 1, LANES), jnp.float32),
            dma((5,)), dma((4,)), dma((3,)), dma((3,)),
            dma((chunks,)), dma((chunks,)), dma((2, 3, chunks)), dma((2, 3, chunks)),
        ],
        compiler_params=pltpu.CompilerParams(
            collective_id=0, has_side_effects=True, vmem_limit_bytes=56 * 1024 * 1024
        ),
    )(
        tall(param), tall(first_moment), tall(second_moment), tall(grad), tall(saved_param),
        owner, generator,
    )
    return tuple(o.reshape(shape) for o in outs)


def solution(mesh):
    split = P("parity", "fsdp")
    return jax.shard_map(
        shards, mesh=mesh, in_specs=(split,) * 5 + (P(), P()), out_specs=(split,) * 4, check_vma=False
    )
```

```python
import functools

import jax
import jax.numpy as jnp
from jax import lax
from jax.experimental import pallas as pl
from jax.experimental.pallas import tpu as pltpu
from jax.sharding import PartitionSpec as P

MESH = pl.DeviceIdType.MESH
NY, NZ = 4, 32
HALF = NZ // 2
REACH = NZ // 4
STRIDE = REACH // 2
PLANE = 32
LANES = 128
CHUNKS = 4
STARTS = (
    16, 8, 8, 4, 8, 6, 9, 4, 7, 7, 6, 6, 6, 5, 8, 12,
    0, 0, 0, 3, 0, 10, 0, 16, 6, 0, 4, 12, 4, 0, 6, 13,
)


def kernel(
    param, first, second, grad, saved, owner, gen,
    out_param, out_first, out_second, out_rows,
    g_v, gf_v, p_v, m_v, v_v, s_v, np_v, nm_v, nv_v, rows_v, deltas,
    plane_buf, near_buf, far_buf,
    in_sem, out_sem, norm_send, norm_recv,
    z_send, z_recv, y_send, y_recv, known, go,
):
    f = lax.axis_index("fsdp")
    me = lax.axis_index("parity")
    z = (me & 1) * HALF + (f >> 3)
    other = me ^ 1
    rows = p_v.shape[0]
    step = rows // CHUNKS

    loads = [
        pltpu.make_async_copy(src, dst, in_sem.at[i])
        for i, (src, dst) in enumerate(
            ((grad, g_v), (param, p_v), (first, m_v), (second, v_v), (saved, s_v))
        )
    ]
    for load in loads:
        load.start()

    def along_z(k):
        t = (z + (k + NZ)) & (NZ - 1)
        return ((t & (HALF - 1)) * 8 + (f & 7), (me & 6) | (t >> 4))

    def along_y(d):
        return (f, (me + 2 * d) & 7)

    mine = (me >> 1) * 8 + (f & 7)

    def in_plane(j):
        return (f ^ (j & 7), me ^ ((j >> 3) * 2))

    def member(bits):
        word = bits - (1 << NZ) if bits >> (NZ - 1) else bits
        return ((jnp.int32(word) >> z) & 1) == 1

    def signal(sem, device):
        pl.semaphore_signal(sem, inc=1, device_id=device, device_id_type=MESH)

    def await_bytes(ref, sem):
        pltpu.make_async_copy(ref, ref, sem).wait()

    barrier = pltpu.get_barrier_semaphore()
    for k in range(STRIDE, 0, -1):
        signal(barrier, along_z(k))
        signal(barrier, along_z(-k))
    for j in range(PLANE - 1, 0, -1):
        signal(barrier, in_plane(j))

    loads[0].wait()
    g = g_v[...].astype(jnp.float32).reshape(rows, LANES)
    gf_v[...] = g
    plane_buf[mine] = jnp.sum(g * g, axis=0, keepdims=True)
    pl.semaphore_wait(barrier, 2 * STRIDE + PLANE - 1)
    for j in range(PLANE - 1, 0, -1):
        pltpu.make_async_remote_copy(
            src_ref=plane_buf.at[mine], dst_ref=plane_buf.at[mine],
            send_sem=norm_send.at[0], recv_sem=norm_recv.at[0],
            device_id=in_plane(j), device_id_type=MESH,
        ).start()
    signal(known, along_z(STRIDE))
    signal(known, along_z(-STRIDE))
    await_bytes(plane_buf.at[pl.ds(0, PLANE - 1)], norm_recv.at[0])

    near_buf[REACH - 1] = jnp.sum(plane_buf[...], axis=0)
    pl.semaphore_wait(known, 2)
    for k in (REACH, *(s * d for d in range(REACH - 1, 0, -1) for s in (1, -1))):
        pltpu.make_async_remote_copy(
            src_ref=near_buf.at[REACH - 1], dst_ref=near_buf.at[REACH - 1 + k],
            send_sem=norm_send.at[1], recv_sem=norm_recv.at[1],
            device_id=along_z(-k), device_id_type=MESH,
        ).start()
    await_bytes(near_buf.at[pl.ds(0, 2 * REACH - 1)], norm_recv.at[1])
    far_buf[0] = jnp.sum(near_buf[REACH - 1 :], axis=0)
    far_buf[1] = jnp.sum(near_buf[:REACH], axis=0)
    for i, k in ((0, -REACH), (1, REACH)):
        pltpu.make_async_remote_copy(
            src_ref=far_buf.at[i], dst_ref=far_buf.at[2 + i],
            send_sem=norm_send.at[2], recv_sem=norm_recv.at[2],
            device_id=along_z(k), device_id_type=MESH,
        ).start()
    around = jnp.sum(near_buf[: 2 * REACH - 1], axis=0)
    for load in loads[1:]:
        load.wait()
    await_bytes(far_buf.at[pl.ds(0, 2)], norm_recv.at[2])
    total = jnp.sum(around + far_buf[2] + far_buf[3], axis=1, keepdims=True)
    norm = jnp.sqrt(total)
    factor = jnp.minimum(1.0, 1.0 / (norm + 1e-6))

    def part_of(k):
        return pl.ds(k * step, step)

    def z_copy(k):
        part = deltas.at[me, part_of(k)]
        return pltpu.make_async_remote_copy(
            src_ref=part, dst_ref=part, send_sem=z_send.at[k], recv_sem=z_recv.at[k],
            device_id=along_z(HALF), device_id_type=MESH,
        )

    def y_copy(hop, d, k, slot):
        part = deltas.at[slot, part_of(k)]
        return pltpu.make_async_remote_copy(
            src_ref=part, dst_ref=part,
            send_sem=y_send.at[hop, d - 1, k], recv_sem=y_recv.at[hop, d - 1, k],
            device_id=along_y(d), device_id_type=MESH,
        )

    scale_first = 1.0 / (1.0 - 0.9**10)
    scale_second = 1.0 / (1.0 - 0.95**10)

    def adamw(k):
        part = part_of(k)
        p = p_v[part]
        clipped = gf_v[part] * factor
        new_first = 0.9 * m_v[part] + 0.1 * clipped
        new_second = 0.95 * v_v[part] + 0.05 * clipped * clipped
        update = new_first * scale_first / (jnp.sqrt(new_second * scale_second) + 1e-8) + 0.1 * p
        new_param = p - 0.05 * update
        np_v[part] = new_param
        nm_v[part] = new_first
        nv_v[part] = new_second
        deltas[me, part] = (new_param - s_v[part]).astype(jnp.bfloat16)

    for hops in sorted(set(STARTS) - {0}):
        senders = sum(1 << ((t - hops) % NZ) for t in range(NZ) if STARTS[t] == hops)

        @pl.when(member(senders))
        def _():
            signal(go, along_z(hops))

    waits = member(sum(1 << t for t in range(NZ) if STARTS[t]))
    for k in range(CHUNKS):
        adamw(k)
        pl.when(jnp.logical_not(waits))(z_copy(k).start)
    for k in range(CHUNKS):
        for d in (2, 1, 3):
            y_copy(0, d, k, me).start()
    stores = [
        pltpu.make_async_copy(src, dst, out_sem.at[i])
        for i, (src, dst) in enumerate(
            ((np_v, out_param), (nm_v, out_first), (nv_v, out_second))
        )
    ]

    def row_store(k):
        part = part_of(k)
        return pltpu.make_async_copy(rows_v.at[part], out_rows.at[part], out_sem.at[3 + k])

    for store in stores:
        store.start()

    @pl.when(waits)
    def _():
        pl.semaphore_wait(go, 1)
        for k in range(CHUNKS):
            z_copy(k).start()

    row = owner[me]
    here = [gen[row, (2 * d) + (me & 1)] for d in range(NY)]
    there = [gen[row, (2 * d) + (other & 1)] for d in range(NY)]

    def mix(coefs, half, k):
        part = part_of(k)
        return sum(coefs[d] * deltas[2 * d + half, part].astype(jnp.float32) for d in range(NY))

    for k in range(CHUNKS):
        for d in (1, 2, 3):
            y_copy(0, d, k, me).wait_recv()
        rows_v[part_of(k)] = mix(here, me & 1, k)
    for k in range(CHUNKS):
        z_copy(k).wait_recv()
        for d in (2, 1, 3):
            y_copy(1, d, k, other).start()
    for k in range(CHUNKS):
        for d in (1, 3, 2):
            y_copy(1, d, k, other).wait_recv()
        part = part_of(k)
        rows_v[part] += mix(there, other & 1, k)
        row_store(k).start()
    await_bytes(plane_buf.at[pl.ds(0, PLANE - 1)], norm_send.at[0])
    await_bytes(near_buf.at[pl.ds(0, 2 * REACH - 1)], norm_send.at[1])
    await_bytes(far_buf.at[pl.ds(0, 2)], norm_send.at[2])
    for k in range(CHUNKS):
        z_copy(k).wait_send()
        for d in (1, 2, 3):
            y_copy(0, d, k, me).wait_send()
            y_copy(1, d, k, other).wait_send()
    for store in stores:
        store.wait()
    for k in range(CHUNKS):
        row_store(k).wait()


def finish(*refs):
    for src, dst in zip(refs[:4], refs[4:]):
        dst[...] = src[...]


def shards(param, first_moment, second_moment, grad, saved_param, owner, generator):
    shape = param.shape
    rows = shape[1] // LANES

    def tall(a):
        return a.reshape(rows, LANES)

    f32 = jax.ShapeDtypeStruct((rows, LANES), jnp.float32)
    big = pltpu.VMEM((rows, LANES), jnp.float32)
    dma = pltpu.SemaphoreType.DMA
    regular = pltpu.SemaphoreType.REGULAR
    anywhere = pl.BlockSpec(memory_space=pl.ANY)
    vmem = pl.BlockSpec(memory_space=pltpu.VMEM)
    smem = pl.BlockSpec(memory_space=pltpu.SMEM)
    outs = pl.pallas_call(
        kernel,
        out_shape=[f32] * 4,
        in_specs=[anywhere] * 5 + [smem] * 2,
        out_specs=[anywhere] * 4,
        scratch_shapes=[
            pltpu.VMEM(shape, grad.dtype), *[big] * 9,
            pltpu.VMEM((2 * NY, rows, LANES), jnp.bfloat16),
            pltpu.VMEM((PLANE, 1, LANES), jnp.float32),
            pltpu.VMEM((2 * REACH, 1, LANES), jnp.float32),
            pltpu.VMEM((4, 1, LANES), jnp.float32),
            dma((5,)), dma((3 + CHUNKS,)), dma((3,)), dma((3,)),
            dma((CHUNKS,)), dma((CHUNKS,)), dma((2, 3, CHUNKS)), dma((2, 3, CHUNKS)),
            regular, regular,
        ],
        compiler_params=pltpu.CompilerParams(
            collective_id=0, has_side_effects=True, vmem_limit_bytes=56 * 1024 * 1024
        ),
    )(
        tall(param), tall(first_moment), tall(second_moment), grad, tall(saved_param),
        owner, generator,
    )
    block = pl.BlockSpec((rows // 2, LANES), lambda i: (i, 0))
    outs = pl.pallas_call(
        finish,
        out_shape=[f32] * 4,
        grid=(2,),
        in_specs=[block] * 4,
        out_specs=[block] * 4,
        compiler_params=pltpu.CompilerParams(vmem_limit_bytes=56 * 1024 * 1024),
    )(*outs)
    return tuple(o.reshape(shape) for o in outs)


def solution(mesh):
    split = P("parity", "fsdp")
    return jax.shard_map(
        shards, mesh=mesh, in_specs=(split,) * 5 + (P(), P()), out_specs=(split,) * 4, check_vma=False
    )
```
